256 devices in a mesh: dp: 64 (over y, z, x_lo), tensor: 4 (over x_hi, core).
Axes of the slice: x: 4 (x_hi: 2, x_lo: 2; x = x_hi * 2 + x_lo), y: 4, z: 8, core: 2. Of those that a mesh axis runs over, the one named last changes fastest.
Arguments:
- images: bfloat16 [180224, 1152], P(('dp', 'tensor')), may hold values from -6 to 6
- texts: bfloat16 [180224, 1152], P(('dp', 'tensor')), may hold values from -6 to 6
- logit_scale: float32 [1], replicated, may hold values from 1 to 2
- logit_bias: float32 [1], replicated, may hold values from -2 to 0
Outputs:
- image_grad: float32 [180224, 1152], P(('dp', 'tensor'))
- text_grad: float32 [180224, 1152], P(('dp', 'tensor'))
The draws below stay inside these ranges and needn't reach their ends.
All inputs are finite; a program needn't handle non-finite values.
Results may differ from the reference program's by a relative error of at most 0.0019.
Values may be sent and summed in bfloat16 or wider, within the bound.
A program may use at most 64 MiB of HBM per device.

```python
import math
import jax
import jax.numpy as jnp

D = 1152
ROWS = 704
STEPS = 4
BATCH = 180224


def shard_levels(own_key, dims, shards, smallest, high):
    def one(dim, shards_of):
        draws = jax.random.uniform(jax.random.fold_in(jax.random.fold_in(own_key, 6), dim), (shards_of,), jnp.float32, smallest / len(shards), high / len(shards))
        return jnp.repeat(jnp.exp(draws), dims[dim] // shards_of).reshape((-1,) + (1,) * (len(dims) - dim - 1))

    level = one(*shards[0])
    for cut in shards[1:]:
        level = level * one(*cut)
    return level


def normal_values(stream_key, dims, deviation, limit, cuts=(), held_as=jnp.bfloat16):
    result = deviation * jax.random.normal(stream_key, dims, jnp.float32)
    if cuts:
        result = result * shard_levels(stream_key, dims, cuts, -0.22, 0.18)
    return jnp.clip(result, -limit, limit).astype(held_as)


def setup_inputs(seed: int = 0) -> dict:
    arg_keys = jax.random.split(jax.random.key(seed), 5)
    return {
        "images": normal_values(arg_keys[0], (BATCH, D), 1.0, 6.0, ((0, 256),)),
        "texts": normal_values(arg_keys[1], (BATCH, D), 1.0, 6.0, ((0, 256),)),
        "logit_scale": jnp.clip(jnp.exp(jax.random.uniform(arg_keys[2], (1,), jnp.float32, math.log(1.0), math.log(2.0))), 1.0, 2.0),
        "logit_bias": jnp.clip(jax.random.uniform(arg_keys[3], (1,), jnp.float32, -2.0, 0.0), -2.0, 0.0),
    }


def reference(images, texts, logit_scale, logit_bias):
    blocks = BATCH // ROWS
    image_blocks = images.reshape(blocks, ROWS, D).astype(jnp.float32)
    text_blocks = texts.reshape(blocks, ROWS, D).astype(jnp.float32)
    factor = logit_scale[0] / math.sqrt(D)
    identity = jnp.eye(ROWS, dtype=jnp.float32)
    image_total = jnp.zeros((blocks, ROWS, D), jnp.float32)
    text_total = jnp.zeros((blocks, ROWS, D), jnp.float32)
    for step in range(STEPS):
        partner = jnp.roll(text_blocks, step, axis=0)
        logits = factor * jnp.einsum('prd,pcd->prc', image_blocks, partner) + logit_bias[0]
        weights = jax.nn.sigmoid(logits)
        if step == 0:
            weights = weights - identity
        weights = weights.astype(jnp.bfloat16).astype(jnp.float32)
        image_total = image_total + factor * jnp.einsum('prc,pcd->prd', weights, partner)
        terms = factor * jnp.einsum('prc,prd->pcd', weights, image_blocks)
        text_total = text_total + jnp.roll(terms, -step, axis=0)
    return (image_total.reshape(BATCH, D), text_total.reshape(BATCH, D))
```

```python
import math

import jax
import jax.numpy as jnp
from jax import lax
from jax.experimental import pallas as pl
from jax.experimental.pallas import tpu as pltpu
from jax.sharding import PartitionSpec as P

CHUNKS = 4
X, Y, LOCAL, D1, D1F, EXTRA, TRANSIT, ZIN, D2, D2F = range(10)
F_LOCAL, F_P1, F_RELAY, F_MZ, F_Z, F_P2, F_M2, F_D1, F_D2 = range(9)


def kernel(ndp, x_ref, y_ref, scale_ref, bias_ref, img_ref, txt_ref, buf, acc, load_sem, out_sem, send_sem, recv_sem):
    rows, width = x_ref.shape
    part = rows // CHUNKS
    dp, tensor = lax.axis_index("dp"), lax.axis_index("tensor")
    core, xh, xl = lax.rem(tensor, 2), tensor // 2, lax.rem(dp, 2)
    is_a = core == xh
    is_z = xl == xh
    not_z = jnp.logical_not(is_z)
    is_b = jnp.logical_not(is_a)
    a = is_a.astype(jnp.int32)
    z = is_z.astype(jnp.int32)

    cut = (dp + 1 - 2 * xl, (1 - xh) * 2 + core)
    side = (dp + 1 - 2 * xl, xh * 2 + 1 - core)
    sibling = (dp, xh * 2 + 1 - core)

    def along_z(sign):
        return (lax.rem(dp + 2 * sign + ndp, ndp), tensor)

    z_extra = 1 - 2 * xh
    z_second = 2 * xh - 1
    first_src, second_src = 1 - xh, xh

    loads = [
        pltpu.make_async_copy(x_ref, buf.at[X], load_sem.at[0]),
        pltpu.make_async_copy(y_ref, buf.at[Y], load_sem.at[1]),
    ]
    for load in loads:
        load.start()
    mesh_id = dict(device_id_type=pl.DeviceIdType.MESH)
    barrier = pltpu.get_barrier_semaphore()
    for peer in (cut, side, sibling):
        pl.semaphore_signal(barrier, inc=1, device_id=peer, **mesh_id)

    @pl.when(is_z)
    def _():
        for sign in (1, -1):
            pl.semaphore_signal(barrier, inc=1, device_id=along_z(sign), **mesh_id)

    acc[...] = jnp.zeros_like(acc)
    for load in loads:
        load.wait()

    pl.semaphore_wait(barrier, 3 + 2 * z)

    def span(k):
        return pl.ds(pl.multiple_of(k * part, 16), part)

    def copy(flow, src, dst, peer, k):
        return pltpu.make_async_remote_copy(
            src_ref=buf.at[src, span(k)],
            dst_ref=buf.at[dst, span(k)],
            send_sem=send_sem.at[flow, k],
            recv_sem=recv_sem.at[dst, k],
            device_id=peer,
            **mesh_id,
        )

    def arrive(b, k):
        pltpu.make_async_copy(buf.at[b, span(k)], buf.at[b, span(k)], recv_sem.at[b, k]).wait()

    def sent(flow, k):
        pltpu.make_async_copy(buf.at[X, span(k)], buf.at[X, span(k)], send_sem.at[flow, k]).wait()

    second_from = jnp.where(is_z, ZIN, second_src)

    def each(body):
        lax.fori_loop(0, CHUNKS, lambda k, c: (body(k), c)[1], 0)

    @each
    def _(k):
        @pl.when(is_a)
        def _():
            copy(F_P1, first_src, TRANSIT, cut, k).start()

        @pl.when(is_b)
        def _():
            copy(F_P1, first_src, jnp.where(is_z, EXTRA, TRANSIT), side, k).start()

        @pl.when(is_z)
        def _():
            copy(F_Z, second_src, ZIN, along_z(z_second), k).start()

        @pl.when(jnp.logical_and(not_z, is_b))
        def _():
            copy(F_P2, second_from, D2, cut, k).start()

        copy(F_LOCAL, 1 - core, LOCAL, sibling, k).start()

    def relay_a(k):
        held = jnp.where(is_z, TRANSIT, EXTRA)
        arrive(held, k)
        copy(F_RELAY, held, D1, cut, k).start()

        @pl.when(is_z)
        def _():
            copy(F_MZ, TRANSIT, EXTRA, along_z(z_extra), k).start()

    def relay_b(k):
        arrive(TRANSIT, k)
        copy(F_RELAY, TRANSIT, D1, side, k).start()

        @pl.when(is_z)
        def _():
            arrive(ZIN, k)
            copy(F_P2, ZIN, D2, cut, k).start()

    def second_a(k):
        @pl.when(is_z)
        def _():
            arrive(ZIN, k)

        copy(F_P2, second_from, D2, cut, k).start()
        copy(F_M2, second_from, EXTRA, side, k).start()

    factor = scale_ref[0] / math.sqrt(width)
    bias = bias_ref[0]

    def weigh(s, b, k, own):
        block = buf[b, span(k), :]
        logits = lax.dot_general(buf[s], block, (((1,), (1,)), ((), ())), preferred_element_type=jnp.float32)
        weights = jax.nn.sigmoid(factor * logits + bias)
        row = lax.broadcasted_iota(jnp.int32, weights.shape, 0)
        column = lax.broadcasted_iota(jnp.int32, weights.shape, 1)
        shift = jnp.where(own, k * part, -2 * rows)
        weights = weights - (row == column + shift).astype(jnp.float32)
        acc[s] += jnp.dot(weights.astype(jnp.bfloat16), block, preferred_element_type=jnp.float32)

    def scale_out(s, copy_out):
        for k in range(CHUNKS):
            tile = pl.ds(k * part, part)
            acc[s, tile, :] = acc[s, tile, :] * factor
            copy_out(s, k, True)

    def out_copy(s, k, start):
        tile = pl.ds(k * part, part)

        @pl.when(s == 0)
        def _():
            c = pltpu.make_async_copy(acc.at[0, tile], img_ref.at[tile], out_sem.at[0, k])
            c.start() if start else c.wait()

        @pl.when(s == 1)
        def _():
            c = pltpu.make_async_copy(acc.at[1, tile], txt_ref.at[tile], out_sem.at[1, k])
            c.start() if start else c.wait()

    def step(t, carry):
        @pl.when(jnp.logical_and(is_a, jnp.logical_and(lax.rem(t, 3) == 0, jnp.logical_and(t >= 3, t <= 12))))
        def _():
            relay_a(t // 3 - 1)

        @pl.when(jnp.logical_and(is_b, jnp.logical_or(t == 8, jnp.logical_and(lax.rem(t, 2) == 0, jnp.logical_and(t >= 12, t <= 16)))))
        def _():
            relay_b(jnp.where(t == 8, 0, (t - 10) // 2))

        @pl.when(jnp.logical_and(is_a, t == 20))
        def _():
            each(second_a)

        @pl.when(t == 28)
        def _():
            scale_out(1 - xh, out_copy)

        u1, u2 = t - 12, t - 20
        even = lax.rem(t, 2) == 0
        first, second = 1 - xh, xh
        k = jnp.where(t < 12, lax.rem(t, 4), jnp.where(t < 20, u1 // 2, jnp.where(t < 28, u2 // 2, t - 28)))
        b = jnp.where(t < 4, Y, jnp.where(t < 8, X, jnp.where(t < 12, LOCAL,
            jnp.where(t < 20, jnp.where(even, D2F - a, D1F - a),
            jnp.where(t < 28, jnp.where(even, D1 + a, EXTRA), D2 + a)))))
        s = jnp.where(t < 4, 0, jnp.where(t < 8, 1, jnp.where(t < 12, jnp.where(is_a, first, second),
            jnp.where(t < 20, jnp.where(even, second, first),
            jnp.where(t < 28, jnp.where(even, first, jnp.where(is_a, second, first)), second)))))
        seen = jnp.logical_or(t < 8, jnp.logical_and(b == EXTRA, jnp.logical_and(is_a, not_z)))

        @pl.when(jnp.logical_not(seen))
        def _():
            arrive(b, k)

        @pl.when(b == D1)
        def _():
            copy(F_D1, D1, D1F, sibling, k).start()

        @pl.when(b == D2)
        def _():
            copy(F_D2, D2, D2F, sibling, k).start()

        weigh(s, b, k, t < 8)
        return carry

    lax.fori_loop(0, 8 * CHUNKS, step, 0)
    scale_out(xh, out_copy)

    @each
    def _(k):
        for flow in (F_LOCAL, F_P1, F_RELAY, F_P2, F_D1, F_D2):
            sent(flow, k)

        @pl.when(is_a)
        def _():
            sent(F_M2, k)

        @pl.when(is_z)
        def _():
            sent(F_Z, k)

        @pl.when(jnp.logical_and(is_z, is_a))
        def _():
            sent(F_MZ, k)

    for s in range(2):
        for k in range(CHUNKS):
            out_copy(s, k, False)


def body(images, texts, logit_scale, logit_bias):
    import functools

    rows, width = images.shape
    any_spec = pl.BlockSpec(memory_space=pl.ANY)
    smem = pl.BlockSpec(memory_space=pltpu.SMEM)
    out = jax.ShapeDtypeStruct((rows, width), jnp.float32)
    return pl.pallas_call(
        functools.partial(kernel, lax.axis_size("dp")),
        out_shape=(out, out),
        in_specs=[any_spec, any_spec, smem, smem],
        out_specs=(any_spec, any_spec),
        scratch_shapes=[
            pltpu.VMEM((10, rows, width), jnp.bfloat16),
            pltpu.VMEM((2, rows, width), jnp.float32),
            pltpu.SemaphoreType.DMA((2,)),
            pltpu.SemaphoreType.DMA((2, CHUNKS)),
            pltpu.SemaphoreType.DMA((9, CHUNKS)),
            pltpu.SemaphoreType.DMA((10, CHUNKS)),
        ],
        compiler_params=pltpu.CompilerParams(
            collective_id=0, has_side_effects=True, vmem_limit_bytes=60 << 20
        ),
        cost_estimate=pl.CostEstimate(
            flops=32 * rows * rows * width, bytes_accessed=12 * rows * width, transcendentals=8 * rows * rows
        ),
        name="pairs",
    )(images, texts, logit_scale, logit_bias)


def solution(mesh):
    in_specs = (P(("dp", "tensor"), None), P(("dp", "tensor"), None), P(), P())
    out_specs = (P(("dp", "tensor"), None), P(("dp", "tensor"), None))
    return jax.shard_map(body, mesh=mesh, in_specs=in_specs, out_specs=out_specs, check_vma=False)
```

```python
import functools
import math

import jax
import jax.numpy as jnp
from jax import lax
from jax.experimental import pallas as pl
from jax.experimental.pallas import tpu as pltpu
from jax.sharding import PartitionSpec as P

CHUNKS = 4
X, Y, LOCAL, D1, D1F, EXTRA, TRANSIT, ZIN, D2, D2F = range(10)
F_LOCAL, F_P1, F_RELAY, F_MZ, F_Z, F_P2, F_M2, F_D1, F_D2 = range(9)


def kernel(ndp, x_ref, y_ref, scale_ref, bias_ref, acc, buf, load_sem, send_sem, recv_sem):
    rows, width = x_ref.shape
    part = rows // CHUNKS
    dp, tensor = lax.axis_index("dp"), lax.axis_index("tensor")
    core, xh, xl = lax.rem(tensor, 2), tensor // 2, lax.rem(dp, 2)
    is_a = core == xh
    is_z = xl == xh
    not_z = jnp.logical_not(is_z)
    is_b = jnp.logical_not(is_a)
    a = is_a.astype(jnp.int32)
    z = is_z.astype(jnp.int32)

    cut = (dp + 1 - 2 * xl, (1 - xh) * 2 + core)
    side = (dp + 1 - 2 * xl, xh * 2 + 1 - core)
    sibling = (dp, xh * 2 + 1 - core)

    def along_z(sign):
        return (lax.rem(dp + 2 * sign + ndp, ndp), tensor)

    z_extra = 1 - 2 * xh
    z_second = 2 * xh - 1
    first_src, second_src = 1 - xh, xh

    loads = [
        pltpu.make_async_copy(x_ref, buf.at[X], load_sem.at[0]),
        pltpu.make_async_copy(y_ref, buf.at[Y], load_sem.at[1]),
    ]
    for load in loads:
        load.start()
    mesh_id = dict(device_id_type=pl.DeviceIdType.MESH)
    barrier = pltpu.get_barrier_semaphore()
    for peer in (cut, side, sibling):
        pl.semaphore_signal(barrier, inc=1, device_id=peer, **mesh_id)

    @pl.when(is_z)
    def _():
        for sign in (1, -1):
            pl.semaphore_signal(barrier, inc=1, device_id=along_z(sign), **mesh_id)

    acc[...] = jnp.zeros_like(acc)
    for load in loads:
        load.wait()

    pl.semaphore_wait(barrier, 3 + 2 * z)

    def span(k):
        return pl.ds(pl.multiple_of(k * part, 16), part)

    def copy(flow, src, dst, peer, k):
        return pltpu.make_async_remote_copy(
            src_ref=buf.at[src, span(k)],
            dst_ref=buf.at[dst, span(k)],
            send_sem=send_sem.at[flow, k],
            recv_sem=recv_sem.at[dst, k],
            device_id=peer,
            **mesh_id,
        )

    def arrive(b, k):
        pltpu.make_async_copy(buf.at[b, span(k)], buf.at[b, span(k)], recv_sem.at[b, k]).wait()

    def sent(flow, k):
        pltpu.make_async_copy(buf.at[X, span(k)], buf.at[X, span(k)], send_sem.at[flow, k]).wait()

    second_from = jnp.where(is_z, ZIN, second_src)

    def each(body):
        lax.fori_loop(0, CHUNKS, lambda k, c: (body(k), c)[1], 0)

    @each
    def _(k):
        @pl.when(is_a)
        def _():
            copy(F_P1, first_src, TRANSIT, cut, k).start()

        @pl.when(is_b)
        def _():
            copy(F_P1, first_src, jnp.where(is_z, EXTRA, TRANSIT), side, k).start()

        @pl.when(is_z)
        def _():
            copy(F_Z, second_src, ZIN, along_z(z_second), k).start()

        @pl.when(jnp.logical_and(not_z, is_b))
        def _():
            copy(F_P2, second_from, D2, cut, k).start()

        copy(F_LOCAL, 1 - core, LOCAL, sibling, k).start()

    def relay_a(k):
        held = jnp.where(is_z, TRANSIT, EXTRA)
        arrive(held, k)
        copy(F_RELAY, held, D1, cut, k).start()

        @pl.when(is_z)
        def _():
            copy(F_MZ, TRANSIT, EXTRA, along_z(z_extra), k).start()

    def relay_b(k):
        arrive(TRANSIT, k)
        copy(F_RELAY, TRANSIT, D1, side, k).start()

        @pl.when(is_z)
        def _():
            arrive(ZIN, k)
            copy(F_P2, ZIN, D2, cut, k).start()

    def second_a(k):
        @pl.when(is_z)
        def _():
            arrive(ZIN, k)

        copy(F_P2, second_from, D2, cut, k).start()
        copy(F_M2, second_from, EXTRA, side, k).start()

    factor = scale_ref[0] / math.sqrt(width)
    bias = bias_ref[0]

    def weigh(s, b, rows_of, own):
        block = buf[b, rows_of, :]
        logits = lax.dot_general(buf[s], block, (((1,), (1,)), ((), ())), preferred_element_type=jnp.float32)
        weights = jax.nn.sigmoid(factor * logits + bias)
        if own is not None:
            row = lax.broadcasted_iota(jnp.int32, weights.shape, 0)
            column = lax.broadcasted_iota(jnp.int32, weights.shape, 1)
            weights = weights - (row == column + jnp.where(own, 0, rows)).astype(jnp.float32)
        acc[s] += jnp.dot(weights.astype(jnp.bfloat16), block, preferred_element_type=jnp.float32)

    def both(b, forward_flow):
        def one(k):
            arrive(b, k)
            copy(forward_flow, b, b + 1, sibling, k).start()

        return one

    def at(u, cond, number):
        return pl.when(jnp.logical_and(u == number, cond))

    def unit(u, carry):
        @at(u, is_a, 1)
        def _():
            relay_a(0)

        @at(u, is_a, 2)
        def _():
            relay_a(1)

        @at(u, is_b, 2)
        def _():
            relay_b(0)

        @pl.when(u == 2)
        def _():
            each(lambda k: arrive(LOCAL, k))

        @at(u, is_a, 3)
        def _():
            relay_a(2)
            both(D2, F_D2)(0)
            relay_a(3)

            @pl.when(not_z)
            def _():
                each(second_a)

            both(D2, F_D2)(1)

            @pl.when(is_z)
            def _():
                each(lambda k: arrive(EXTRA, k))

        @at(u, is_b, 3)
        def _():
            relay_b(1)
            relay_b(2)
            relay_b(3)
            each(lambda k: arrive(D2F, k))

        @at(u, is_a, 4)
        def _():
            @pl.when(is_z)
            def _():
                each(second_a)

            both(D2, F_D2)(2)
            both(D2, F_D2)(3)

        @at(u, is_b, 4)
        def _():
            each(lambda k: arrive(D1F, k))

        @pl.when(u == 5)
        def _():
            each(both(D1, F_D1))

        @at(u, is_a, 6)
        def _():
            each(lambda k: arrive(D1F, k))

        @at(u, is_b, 6)
        def _():
            each(lambda k: arrive(EXTRA, k))

        first, second = 1 - xh, xh
        b = jnp.where(u == 0, Y, jnp.where(u == 1, X, jnp.where(u == 2, LOCAL, jnp.where(u == 3,
            jnp.where(is_a, EXTRA, D2F), jnp.where(u == 4, jnp.where(is_a, D2, D1F),
            jnp.where(u == 5, D1, jnp.where(is_a, D1F, EXTRA)))))))
        in_first = jnp.where(u == 2, is_a, jnp.where(u == 3, False, jnp.where(u == 4, is_b, True)))
        s = jnp.where(u == 0, 0, jnp.where(u == 1, 1, jnp.where(in_first, first, second)))
        weigh(s, b, slice(None), u < 2)
        return carry

    lax.fori_loop(0, 7, unit, 0)

    @each
    def _(k):
        @pl.when(is_a)
        def _():
            arrive(D2F, k)

        @pl.when(is_b)
        def _():
            both(D2, F_D2)(k)

        weigh(xh, D2 + a, span(k), None)

    @each
    def _(k):
        for flow in (F_LOCAL, F_P1, F_RELAY, F_P2, F_D1, F_D2):
            sent(flow, k)

        @pl.when(is_a)
        def _():
            sent(F_M2, k)

        @pl.when(is_z)
        def _():
            sent(F_Z, k)

        @pl.when(jnp.logical_and(is_z, is_a))
        def _():
            sent(F_MZ, k)


def body(images, texts, logit_scale, logit_bias):
    rows, width = images.shape
    hbm = pl.BlockSpec(memory_space=pltpu.HBM)
    smem = pl.BlockSpec(memory_space=pltpu.SMEM)
    factor = logit_scale[0] / math.sqrt(width)
    total = pl.pallas_call(
        functools.partial(kernel, lax.axis_size("dp")),
        out_shape=pltpu.VMEM((2, rows, width), jnp.float32),
        in_specs=[hbm, hbm, smem, smem],
        out_specs=pl.BlockSpec(memory_space=pltpu.VMEM),
        scratch_shapes=[
            pltpu.VMEM((10, rows, width), jnp.bfloat16),
            pltpu.SemaphoreType.DMA((2,)),
            pltpu.SemaphoreType.DMA((9, CHUNKS)),
            pltpu.SemaphoreType.DMA((10, CHUNKS)),
        ],
        compiler_params=pltpu.CompilerParams(
            collective_id=0, has_side_effects=True, vmem_limit_bytes=57 << 20
        ),
        cost_estimate=pl.CostEstimate(
            flops=32 * rows * rows * width, bytes_accessed=12 * rows * width, transcendentals=8 * rows * rows
        ),
        name="pairs",
    )(images, texts, logit_scale, logit_bias)
    return (factor * total[0], factor * total[1])


def solution(mesh):
    in_specs = (P(("dp", "tensor"), None), P(("dp", "tensor"), None), P(), P())
    out_specs = (P(("dp", "tensor"), None), P(("dp", "tensor"), None))
    return jax.shard_map(body, mesh=mesh, in_specs=in_specs, out_specs=out_specs, check_vma=False)
```

```python
import functools
import math

import jax
import jax.numpy as jnp
from jax import lax
from jax.experimental import pallas as pl
from jax.experimental.pallas import tpu as pltpu
from jax.sharding import PartitionSpec as P

CHUNKS = 4
TILES = 4
X, Y, LOCAL, D1, D1F, EXTRA, TRANSIT, ZIN, D2, D2F = range(10)
F_LOCAL, F_P1, F_RELAY, F_MZ, F_Z, F_P2, F_M2, F_D1, F_D2 = range(9)


def kernel(ndp, x_ref, y_ref, scale_ref, bias_ref, acc, buf, load_sem, send_sem, recv_sem, ready):
    rows, width = x_ref.shape
    part = rows // CHUNKS
    dp, tensor = lax.axis_index("dp"), lax.axis_index("tensor")
    core, xh, xl = lax.rem(tensor, 2), tensor // 2, lax.rem(dp, 2)
    is_a = core == xh
    is_z = xl == xh
    not_z = jnp.logical_not(is_z)
    is_b = jnp.logical_not(is_a)
    a = is_a.astype(jnp.int32)
    z = is_z.astype(jnp.int32)

    cut = (dp + 1 - 2 * xl, (1 - xh) * 2 + core)
    side = (dp + 1 - 2 * xl, xh * 2 + 1 - core)
    sibling = (dp, xh * 2 + 1 - core)

    def along_z(sign):
        return (lax.rem(dp + 2 * sign + ndp, ndp), tensor)

    z_extra = 1 - 2 * xh
    z_second = 2 * xh - 1
    first_src, second_src = 1 - xh, xh

    loads = [
        pltpu.make_async_copy(x_ref, buf.at[X], load_sem.at[0]),
        pltpu.make_async_copy(y_ref, buf.at[Y], load_sem.at[1]),
    ]
    for load in loads:
        load.start()
    mesh_id = dict(device_id_type=pl.DeviceIdType.MESH)
    barrier = pltpu.get_barrier_semaphore()
    for peer in (cut, side, sibling):
        pl.semaphore_signal(barrier, inc=1, device_id=peer, **mesh_id)

    @pl.when(is_z)
    def _():
        for sign in (1, -1):
            pl.semaphore_signal(barrier, inc=1, device_id=(along_z(sign)[0], xh * 2 + 1 - xh), **mesh_id)

    acc[...] = jnp.zeros_like(acc)
    for load in loads:
        load.wait()

    pl.semaphore_wait(barrier, 3 + 4 * z * (1 - a))

    @pl.when(jnp.logical_and(is_z, is_b))
    def _():
        pl.semaphore_signal(ready, inc=1, device_id=sibling, **mesh_id)

    def span(k):
        return pl.ds(pl.multiple_of(k * part, 16), part)

    def copy(flow, src, dst, peer, k):
        return pltpu.make_async_remote_copy(
            src_ref=buf.at[src, span(k)],
            dst_ref=buf.at[dst, span(k)],
            send_sem=send_sem.at[flow, k],
            recv_sem=recv_sem.at[dst, k],
            device_id=peer,
            **mesh_id,
        )

    def arrive(b, k):
        pltpu.make_async_copy(buf.at[b, span(k)], buf.at[b, span(k)], recv_sem.at[b, k]).wait()

    def sent(flow, k):
        pltpu.make_async_copy(buf.at[X, span(k)], buf.at[X, span(k)], send_sem.at[flow, k]).wait()

    second_from = jnp.where(is_z, ZIN, second_src)

    def each(body):
        lax.fori_loop(0, CHUNKS, lambda k, c: (body(k), c)[1], 0)

    def send_z(k):
        copy(F_Z, second_src, ZIN, along_z(z_second), k).start()

    @each
    def _(k):
        @pl.when(is_a)
        def _():
            copy(F_P1, first_src, TRANSIT, cut, k).start()

        @pl.when(is_b)
        def _():
            copy(F_P1, first_src, jnp.where(is_z, EXTRA, TRANSIT), side, k).start()

        @pl.when(jnp.logical_and(is_z, is_b))
        def _():
            send_z(k)

        @pl.when(jnp.logical_and(not_z, is_b))
        def _():
            copy(F_P2, second_from, D2, cut, k).start()

        copy(F_LOCAL, 1 - core, LOCAL, sibling, k).start()

    def relay_a(k):
        held = jnp.where(is_z, TRANSIT, EXTRA)
        arrive(held, k)
        copy(F_RELAY, held, D1, cut, k).start()

        @pl.when(is_z)
        def _():
            copy(F_MZ, TRANSIT, EXTRA, along_z(z_extra), k).start()

    def relay_b(k):
        arrive(TRANSIT, k)
        copy(F_RELAY, TRANSIT, D1, side, k).start()

        @pl.when(is_z)
        def _():
            arrive(ZIN, k)
            copy(F_P2, ZIN, D2, cut, k).start()

    def second_a(k):
        @pl.when(is_z)
        def _():
            arrive(ZIN, k)

        copy(F_P2, second_from, D2, cut, k).start()
        copy(F_M2, second_from, EXTRA, side, k).start()

    factor = scale_ref[0] / math.sqrt(width)
    bias = bias_ref[0]

    def weigh(s, b, rows_of, own):
        block = buf[b, rows_of, :]
        logits = lax.dot_general(buf[s], block, (((1,), (1,)), ((), ())), preferred_element_type=jnp.float32)
        weights = jax.nn.sigmoid(factor * logits + bias)
        if own is not None:
            row = lax.broadcasted_iota(jnp.int32, weights.shape, 0)
            column = lax.broadcasted_iota(jnp.int32, weights.shape, 1)
            weights = weights - (row == column + jnp.where(own, 0, rows)).astype(jnp.float32)
        acc[s] += jnp.dot(weights.astype(jnp.bfloat16), block, preferred_element_type=jnp.float32)

    def both(b, forward_flow):
        def one(k):
            arrive(b, k)
            copy(forward_flow, b, b + 1, sibling, k).start()

        return one

    def at(u, cond, number):
        return pl.when(jnp.logical_and(u == number, cond))

    def unit(u, carry):
        @at(u, is_a, 1)
        def _():
            @pl.when(is_z)
            def _():
                pl.semaphore_wait(ready, 1)
                each(send_z)

            relay_a(0)

        @at(u, is_a, 2)
        def _():
            relay_a(1)

        @at(u, is_b, 2)
        def _():
            relay_b(0)

        @pl.when(u == 2)
        def _():
            each(lambda k: arrive(LOCAL, k))

        @at(u, is_a, 3)
        def _():
            relay_a(2)
            both(D2, F_D2)(0)
            relay_a(3)

            @pl.when(not_z)
            def _():
                each(second_a)

            both(D2, F_D2)(1)

            @pl.when(is_z)
            def _():
                each(lambda k: arrive(EXTRA, k))

        @at(u, is_b, 3)
        def _():
            relay_b(1)
            relay_b(2)
            relay_b(3)
            each(lambda k: arrive(D2F, k))

        @at(u, is_a, 4)
        def _():
            @pl.when(is_z)
            def _():
                each(second_a)

            both(D2, F_D2)(2)
            both(D2, F_D2)(3)

        @at(u, is_b, 4)
        def _():
            each(lambda k: arrive(D1F, k))

        @pl.when(u == 5)
        def _():
            each(both(D1, F_D1))

        @at(u, is_a, 6)
        def _():
            each(lambda k: arrive(D1F, k))

        @at(u, is_b, 6)
        def _():
            each(lambda k: arrive(EXTRA, k))

        first, second = 1 - xh, xh
        b = jnp.where(u == 0, Y, jnp.where(u == 1, X, jnp.where(u == 2, LOCAL, jnp.where(u == 3,
            jnp.where(is_a, EXTRA, D2F), jnp.where(u == 4, jnp.where(is_a, D2, D1F),
            jnp.where(u == 5, D1, jnp.where(is_a, D1F, EXTRA)))))))
        in_first = jnp.where(u == 2, is_a, jnp.where(u == 3, False, jnp.where(u == 4, is_b, True)))
        s = jnp.where(u == 0, 0, jnp.where(u == 1, 1, jnp.where(in_first, first, second)))
        weigh(s, b, slice(None), u < 2)
        return carry

    lax.fori_loop(0, 7, unit, 0)

    acc[1 - xh] = acc[1 - xh] * factor

    @each
    def _(k):
        @pl.when(is_a)
        def _():
            arrive(D2F, k)

        @pl.when(is_b)
        def _():
            both(D2, F_D2)(k)

        @pl.when(k < CHUNKS - 1)
        def _():
            weigh(xh, D2 + a, span(k), None)

    @each
    def _(k):
        for flow in (F_LOCAL, F_P1, F_RELAY, F_P2, F_D1, F_D2):
            sent(flow, k)

        @pl.when(is_a)
        def _():
            sent(F_M2, k)

        @pl.when(is_z)
        def _():
            sent(F_Z, k)

        @pl.when(jnp.logical_and(is_z, is_a))
        def _():
            sent(F_MZ, k)


def finish(acc, buf, scale_ref, bias_ref, img_ref, txt_ref, result, sem):
    rows, width = img_ref.shape
    part = rows // CHUNKS
    tile = rows // TILES
    tensor = lax.axis_index("tensor")
    core, xh = lax.rem(tensor, 2), tensor // 2
    factor = scale_ref[0] / math.sqrt(width)
    bias = bias_ref[0]

    def write(src, dst, number):
        return pltpu.make_async_copy(src, dst, sem.at[number])

    def first(start):
        for s, ref in ((0, img_ref), (1, txt_ref)):
            @pl.when(xh == 1 - s)
            def _():
                c = write(acc.at[s], ref, 0)
                c.start() if start else c.wait()

    def second(m, start):
        span = pl.ds(m * tile, tile)
        for s, ref in ((0, img_ref), (1, txt_ref)):
            @pl.when(xh == s)
            def _():
                c = write(result.at[span], ref.at[span], 1 + m)
                c.start() if start else c.wait()

    first(True)
    block = buf[D2 + (core == xh).astype(jnp.int32), rows - part :, :]
    for m in range(TILES):
        span = pl.ds(m * tile, tile)
        logits = lax.dot_general(buf[xh, span, :], block, (((1,), (1,)), ((), ())), preferred_element_type=jnp.float32)
        weights = jax.nn.sigmoid(factor * logits + bias).astype(jnp.bfloat16)
        result[span, :] = factor * (acc[xh, span, :] + jnp.dot(weights, block, preferred_element_type=jnp.float32))
        second(m, True)
    first(False)
    for m in range(TILES):
        second(m, False)


def body(images, texts, logit_scale, logit_bias):
    rows, width = images.shape
    hbm = pl.BlockSpec(memory_space=pltpu.HBM)
    smem = pl.BlockSpec(memory_space=pltpu.SMEM)
    vmem = pl.BlockSpec(memory_space=pltpu.VMEM)
    out = jax.ShapeDtypeStruct((rows, width), jnp.float32)
    total, blocks = pl.pallas_call(
        functools.partial(kernel, lax.axis_size("dp")),
        out_shape=(pltpu.VMEM((2, rows, width), jnp.float32), pltpu.VMEM((10, rows, width), jnp.bfloat16)),
        in_specs=[hbm, hbm, smem, smem],
        out_specs=(vmem, vmem),
        scratch_shapes=[
            pltpu.SemaphoreType.DMA((2,)),
            pltpu.SemaphoreType.DMA((9, CHUNKS)),
            pltpu.SemaphoreType.DMA((10, CHUNKS)),
            pltpu.SemaphoreType.REGULAR,
        ],
        compiler_params=pltpu.CompilerParams(
            collective_id=0, has_side_effects=True, vmem_limit_bytes=41 << 20
        ),
        cost_estimate=pl.CostEstimate(
            flops=32 * rows * rows * width, bytes_accessed=12 * rows * width, transcendentals=8 * rows * rows
        ),
        name="pairs",
    )(images, texts, logit_scale, logit_bias)
    return pl.pallas_call(
        finish,
        out_shape=(out, out),
        in_specs=[vmem, vmem, smem, smem],
        out_specs=(hbm, hbm),
        scratch_shapes=[pltpu.VMEM((rows, width), jnp.float32), pltpu.SemaphoreType.DMA((1 + TILES,))],
        compiler_params=pltpu.CompilerParams(vmem_limit_bytes=41 << 20),
        name="finish",
    )(
        pltpu.with_memory_space_constraint(total, pltpu.VMEM),
        pltpu.with_memory_space_constraint(blocks, pltpu.VMEM),
        logit_scale,
        logit_bias,
    )


def solution(mesh):
    in_specs = (P(("dp", "tensor"), None), P(("dp", "tensor"), None), P(), P())
    out_specs = (P(("dp", "tensor"), None), P(("dp", "tensor"), None))
    return jax.shard_map(body, mesh=mesh, in_specs=in_specs, out_specs=out_specs, check_vma=False)
```

```python
import functools
import math

import jax
import jax.numpy as jnp
from jax import lax
from jax.experimental import pallas as pl
from jax.experimental.pallas import tpu as pltpu
from jax.sharding import PartitionSpec as P

CHUNKS = 4
TILES = 4
X, Y, LOCAL, D1, D1F, EXTRA, TRANSIT, ZIN, D2, D2F = range(10)
F_LOCAL, F_P1, F_RELAY, F_MZ, F_Z, F_P2, F_M2, F_D1, F_D2 = range(9)


def kernel(ndp, x_ref, y_ref, scale_ref, bias_ref, acc, buf, load_sem, send_sem, recv_sem, ready):
    rows, width = x_ref.shape
    part = rows // CHUNKS
    dp, tensor = lax.axis_index("dp"), lax.axis_index("tensor")
    core, xh, xl = lax.rem(tensor, 2), tensor // 2, lax.rem(dp, 2)
    is_a = core == xh
    is_z = xl == xh
    not_z = jnp.logical_not(is_z)
    is_b = jnp.logical_not(is_a)
    a = is_a.astype(jnp.int32)
    z = is_z.astype(jnp.int32)

    cut = (dp + 1 - 2 * xl, (1 - xh) * 2 + core)
    side = (dp + 1 - 2 * xl, xh * 2 + 1 - core)
    sibling = (dp, xh * 2 + 1 - core)

    def along_z(sign):
        return (lax.rem(dp + 2 * sign + ndp, ndp), tensor)

    z_extra = 1 - 2 * xh
    z_second = 2 * xh - 1
    first_src, second_src = 1 - xh, xh

    loads = [
        pltpu.make_async_copy(x_ref, buf.at[X], load_sem.at[0]),
        pltpu.make_async_copy(y_ref, buf.at[Y], load_sem.at[1]),
    ]
    for load in loads:
        load.start()
    mesh_id = dict(device_id_type=pl.DeviceIdType.MESH)
    barrier = pltpu.get_barrier_semaphore()
    for peer in (cut, side, sibling):
        pl.semaphore_signal(barrier, inc=1, device_id=peer, **mesh_id)

    @pl.when(is_z)
    def _():
        for sign in (1, -1):
            pl.semaphore_signal(barrier, inc=1, device_id=(along_z(sign)[0], xh * 2 + 1 - xh), **mesh_id)

    acc[...] = jnp.zeros_like(acc)
    for load in loads:
        load.wait()

    pl.semaphore_wait(barrier, 3 + 4 * z * (1 - a))

    @pl.when(jnp.logical_and(is_z, is_b))
    def _():
        pl.semaphore_signal(ready, inc=1, device_id=sibling, **mesh_id)

    def span(k):
        return pl.ds(pl.multiple_of(k * part, 16), part)

    def copy(flow, src, dst, peer, k):
        return pltpu.make_async_remote_copy(
            src_ref=buf.at[src, span(k)],
            dst_ref=buf.at[dst, span(k)],
            send_sem=send_sem.at[flow, k],
            recv_sem=recv_sem.at[dst, k],
            device_id=peer,
            **mesh_id,
        )

    def arrive(b, k):
        pltpu.make_async_copy(buf.at[b, span(k)], buf.at[b, span(k)], recv_sem.at[b, k]).wait()

    def sent(flow, k):
        pltpu.make_async_copy(buf.at[X, span(k)], buf.at[X, span(k)], send_sem.at[flow, k]).wait()

    second_from = jnp.where(is_z, ZIN, second_src)

    def each(body):
        lax.fori_loop(0, CHUNKS, lambda k, c: (body(k), c)[1], 0)

    def send_z(k):
        copy(F_Z, second_src, ZIN, along_z(z_second), k).start()

    @each
    def _(k):
        @pl.when(is_a)
        def _():
            copy(F_P1, first_src, TRANSIT, cut, k).start()

        @pl.when(is_b)
        def _():
            copy(F_P1, first_src, jnp.where(is_z, EXTRA, TRANSIT), side, k).start()

        @pl.when(jnp.logical_and(is_z, is_b))
        def _():
            send_z(k)

        @pl.when(jnp.logical_and(not_z, is_b))
        def _():
            copy(F_P2, second_from, D2, cut, k).start()

        copy(F_LOCAL, 1 - core, LOCAL, sibling, k).start()

    def relay_a(k):
        held = jnp.where(is_z, TRANSIT, EXTRA)
        arrive(held, k)
        copy(F_RELAY, held, D1, cut, k).start()

        @pl.when(is_z)
        def _():
            copy(F_MZ, TRANSIT, EXTRA, along_z(z_extra), k).start()

    def relay_b(k):
        arrive(TRANSIT, k)
        copy(F_RELAY, TRANSIT, D1, side, k).start()

    def second_b(k):
        arrive(ZIN, k)
        copy(F_P2, ZIN, D2, cut, k).start()

    def second_a(k):
        @pl.when(is_z)
        def _():
            arrive(ZIN, k)

        copy(F_P2, second_from, D2, cut, k).start()
        copy(F_M2, second_from, EXTRA, side, k).start()

    factor = scale_ref[0] / math.sqrt(width)
    bias = bias_ref[0]

    def weigh(s, b, rows_of, own, offset=0):
        block = buf[b, rows_of, :]
        logits = lax.dot_general(buf[s], block, (((1,), (1,)), ((), ())), preferred_element_type=jnp.float32)
        weights = jax.nn.sigmoid(factor * logits + bias)
        if own is not None:
            row = lax.broadcasted_iota(jnp.int32, weights.shape, 0)
            column = lax.broadcasted_iota(jnp.int32, weights.shape, 1)
            weights = weights - (row == column + jnp.where(own, offset, rows)).astype(jnp.float32)
        acc[s] += jnp.dot(weights.astype(jnp.bfloat16), block, preferred_element_type=jnp.float32)

    def both(b, forward_flow):
        def one(k):
            arrive(b, k)
            copy(forward_flow, b, b + 1, sibling, k).start()

        return one

    forward_1, forward_2 = both(D1, F_D1), both(D2, F_D2)

    def arrive_half(b, h):
        for k in range(h * CHUNKS // 2, (h + 1) * CHUNKS // 2):
            arrive(b, k)

    def before(cond, number):
        return lambda body: plans.append((cond, number, body))

    plans = []

    a_z, b_z = jnp.logical_and(is_a, is_z), jnp.logical_and(is_b, is_z)
    b_n = jnp.logical_and(is_b, not_z)

    @before(a_z, 2)
    def _():
        pl.semaphore_wait(ready, 1)
        each(send_z)

    @before(is_a, 2)
    def _():
        relay_a(0)

    @before(is_a, 4)
    def _():
        relay_a(1)

    @before(is_b, 4)
    def _():
        relay_b(0)

    @before(True, 4)
    def _():
        each(lambda k: arrive(LOCAL, k))

    @before(b_z, 5)
    def _():
        second_b(0)

    @before(is_a, 6)
    def _():
        relay_a(2)
        relay_a(3)

    @before(jnp.logical_and(is_a, not_z), 6)
    def _():
        each(second_a)

    @before(is_a, 6)
    def _():
        forward_1(0)
        forward_1(1)

    @before(b_n, 6)
    def _():
        relay_b(1)
        relay_b(2)
        relay_b(3)

    @before(b_z, 6)
    def _():
        relay_b(1)
        second_b(1)
        relay_b(2)
        relay_b(3)
        second_b(2)

    @before(is_b, 6)
    def _():
        arrive_half(D1F, 0)

    @before(a_z, 7)
    def _():
        arrive_half(EXTRA, 0)

    @before(is_a, 7)
    def _():
        forward_2(0)

    @before(b_z, 7)
    def _():
        arrive_half(EXTRA, 0)

    @before(b_n, 7)
    def _():
        arrive_half(D2F, 0)

    @before(a_z, 8)
    def _():
        second_a(0)
        second_a(1)

    @before(is_a, 8)
    def _():
        forward_2(1)

    @before(b_z, 8)
    def _():
        second_b(3)
        arrive_half(D2F, 0)

    @before(b_n, 8)
    def _():
        arrive_half(D1F, 1)

    @before(a_z, 9)
    def _():
        arrive_half(EXTRA, 1)
        second_a(2)

    @before(b_z, 9)
    def _():
        arrive_half(EXTRA, 1)

    @before(b_n, 9)
    def _():
        arrive_half(D2F, 1)

    @before(a_z, 10)
    def _():
        second_a(3)

    @before(is_a, 10)
    def _():
        forward_1(2)

    @before(is_a, 10)
    def _():
        forward_2(2)
        forward_1(3)

    @before(b_z, 10)
    def _():
        arrive_half(D1F, 1)

    @before(b_n, 10)
    def _():
        forward_1(0)
        forward_1(1)

    @before(is_a, 11)
    def _():
        forward_2(3)

    @before(b_z, 11)
    def _():
        forward_1(0)
        forward_1(1)

    @before(b_n, 11)
    def _():
        arrive_half(EXTRA, 0)

    @before(is_a, 12)
    def _():
        arrive_half(D1F, 0)

    @before(b_z, 12)
    def _():
        arrive_half(D2F, 1)

    @before(b_n, 12)
    def _():
        forward_1(2)
        forward_1(3)

    @before(is_a, 13)
    def _():
        arrive_half(D1F, 1)

    @before(b_z, 13)
    def _():
        forward_1(2)
        forward_1(3)

    @before(b_n, 13)
    def _():
        arrive_half(EXTRA, 1)

    first, second = 1 - xh, xh
    opening = [(Y, 0, 0), (Y, 1, 0), (X, 0, 1), (X, 1, 1)]
    units_a = opening + [(LOCAL, 0, first), (LOCAL, 1, first), (D1, 0, first), (EXTRA, 0, second),
                         (D2, 0, second), (EXTRA, 1, second), (D1, 1, first), (D2, 1, second),
                         (D1F, 0, first), (D1F, 1, first)]
    units_bz = opening + [(LOCAL, 0, second), (LOCAL, 1, second), (D1F, 0, first), (EXTRA, 0, first),
                          (D2F, 0, second), (EXTRA, 1, first), (D1F, 1, first), (D1, 0, first),
                          (D2F, 1, second), (D1, 1, first)]
    units_bn = opening + [(LOCAL, 0, second), (LOCAL, 1, second), (D1F, 0, first), (D2F, 0, second),
                          (D1F, 1, first), (D2F, 1, second), (D1, 0, first), (EXTRA, 0, first),
                          (D1, 1, first), (EXTRA, 1, first)]
    half = rows // 2

    def unit(u, carry):
        for cond, number, plan in plans:
            pl.when(jnp.logical_and(u == number, cond))(plan)

        def pick(field):
            value = jnp.int32(0)
            for number, (ua, ubz, ubn) in enumerate(zip(units_a, units_bz, units_bn)):
                which = jnp.where(is_a, ua[field], jnp.where(is_z, ubz[field], ubn[field]))
                value = jnp.where(u == number, which, value)
            return value

        h = pick(1)
        weigh(pick(2), pick(0), pl.ds(pl.multiple_of(h * half, 16), half), u < 4, h * half)
        return carry

    lax.fori_loop(0, len(units_a), unit, 0)
    acc[1 - xh] = acc[1 - xh] * factor

    @each
    def _(k):
        @pl.when(is_a)
        def _():
            arrive(D2F, k)

        @pl.when(is_b)
        def _():
            forward_2(k)

        @pl.when(k < CHUNKS - 1)
        def _():
            weigh(xh, D2 + a, span(k), None)

    @each
    def _(k):
        for flow in (F_LOCAL, F_P1, F_RELAY, F_P2, F_D1, F_D2):
            sent(flow, k)

        @pl.when(is_a)
        def _():
            sent(F_M2, k)

        @pl.when(is_z)
        def _():
            sent(F_Z, k)

        @pl.when(jnp.logical_and(is_z, is_a))
        def _():
            sent(F_MZ, k)


def finish(acc, buf, scale_ref, bias_ref, img_ref, txt_ref, result, sem):
    rows, width = img_ref.shape
    part = rows // CHUNKS
    tile = rows // TILES
    tensor = lax.axis_index("tensor")
    core, xh = lax.rem(tensor, 2), tensor // 2
    factor = scale_ref[0] / math.sqrt(width)
    bias = bias_ref[0]

    def write(src, dst, number):
        return pltpu.make_async_copy(src, dst, sem.at[number])

    def first(start):
        for s, ref in ((0, img_ref), (1, txt_ref)):
            @pl.when(xh == 1 - s)
            def _():
                c = write(acc.at[s], ref, 0)
                c.start() if start else c.wait()

    def second(m, start):
        span = pl.ds(m * tile, tile)
        for s, ref in ((0, img_ref), (1, txt_ref)):
            @pl.when(xh == s)
            def _():
                c = write(result.at[span], ref.at[span], 1 + m)
                c.start() if start else c.wait()

    first(True)
    block = buf[D2 + (core == xh).astype(jnp.int32), rows - part :, :]
    for m in range(TILES):
        span = pl.ds(m * tile, tile)
        logits = lax.dot_general(buf[xh, span, :], block, (((1,), (1,)), ((), ())), preferred_element_type=jnp.float32)
        weights = jax.nn.sigmoid(factor * logits + bias).astype(jnp.bfloat16)
        result[span, :] = factor * (acc[xh, span, :] + jnp.dot(weights, block, preferred_element_type=jnp.float32))
        second(m, True)
    first(False)
    for m in range(TILES):
        second(m, False)


def body(images, texts, logit_scale, logit_bias):
    rows, width = images.shape
    hbm = pl.BlockSpec(memory_space=pltpu.HBM)
    smem = pl.BlockSpec(memory_space=pltpu.SMEM)
    vmem = pl.BlockSpec(memory_space=pltpu.VMEM)
    out = jax.ShapeDtypeStruct((rows, width), jnp.float32)
    total, blocks = pl.pallas_call(
        functools.partial(kernel, lax.axis_size("dp")),
        out_shape=(pltpu.VMEM((2, rows, width), jnp.float32), pltpu.VMEM((10, rows, width), jnp.bfloat16)),
        in_specs=[hbm, hbm, smem, smem],
        out_specs=(vmem, vmem),
        scratch_shapes=[
            pltpu.SemaphoreType.DMA((2,)),
            pltpu.SemaphoreType.DMA((9, CHUNKS)),
            pltpu.SemaphoreType.DMA((10, CHUNKS)),
            pltpu.SemaphoreType.REGULAR,
        ],
        compiler_params=pltpu.CompilerParams(
            collective_id=0, has_side_effects=True, vmem_limit_bytes=41 << 20
        ),
        cost_estimate=pl.CostEstimate(
            flops=32 * rows * rows * width, bytes_accessed=12 * rows * width, transcendentals=8 * rows * rows
        ),
        name="pairs",
    )(images, texts, logit_scale, logit_bias)
    return pl.pallas_call(
        finish,
        out_shape=(out, out),
        in_specs=[vmem, vmem, smem, smem],
        out_specs=(hbm, hbm),
        scratch_shapes=[pltpu.VMEM((rows, width), jnp.float32), pltpu.SemaphoreType.DMA((1 + TILES,))],
        compiler_params=pltpu.CompilerParams(vmem_limit_bytes=41 << 20),
        name="finish",
    )(
        pltpu.with_memory_space_constraint(total, pltpu.VMEM),
        pltpu.with_memory_space_constraint(blocks, pltpu.VMEM),
        logit_scale,
        logit_bias,
    )


def solution(mesh):
    in_specs = (P(("dp", "tensor"), None), P(("dp", "tensor"), None), P(), P())
    out_specs = (P(("dp", "tensor"), None), P(("dp", "tensor"), None))
    return jax.shard_map(body, mesh=mesh, in_specs=in_specs, out_specs=out_specs, check_vma=False)
```

```python
import functools
import math

import jax
import jax.numpy as jnp
from jax import lax
from jax.experimental import pallas as pl
from jax.experimental.pallas import tpu as pltpu
from jax.sharding import PartitionSpec as P

CHUNKS = 4
TILES = 4
X, Y, LOCAL, D1, D1F, EXTRA, TRANSIT, ZIN, D2, D2F = range(10)
F_LOCAL, F_P1, F_RELAY, F_MZ, F_Z, F_P2, F_M2, F_D1, F_D2 = range(9)


def kernel(ndp, x_ref, y_ref, scale_ref, bias_ref, acc, buf, load_sem, send_sem, recv_sem, ready):
    rows, width = x_ref.shape
    part = rows // CHUNKS
    dp, tensor = lax.axis_index("dp"), lax.axis_index("tensor")
    core, xh, xl = lax.rem(tensor, 2), tensor // 2, lax.rem(dp, 2)
    is_a = core == xh
    is_z = xl == xh
    not_z = jnp.logical_not(is_z)
    is_b = jnp.logical_not(is_a)
    a = is_a.astype(jnp.int32)
    z = is_z.astype(jnp.int32)

    cut = (dp + 1 - 2 * xl, (1 - xh) * 2 + core)
    side = (dp + 1 - 2 * xl, xh * 2 + 1 - core)
    sibling = (dp, xh * 2 + 1 - core)

    def along_z(sign):
        return (lax.rem(dp + 2 * sign + ndp, ndp), tensor)

    z_extra = 1 - 2 * xh
    z_second = 2 * xh - 1
    first_src, second_src = 1 - xh, xh

    loads = [
        pltpu.make_async_copy(x_ref, buf.at[X], load_sem.at[0]),
        pltpu.make_async_copy(y_ref, buf.at[Y], load_sem.at[1]),
    ]
    for load in loads:
        load.start()
    mesh_id = dict(device_id_type=pl.DeviceIdType.MESH)
    barrier = pltpu.get_barrier_semaphore()
    a_z, b_z = jnp.logical_and(is_a, is_z), jnp.logical_and(is_b, is_z)
    b_n = jnp.logical_and(is_b, not_z)

    pl.semaphore_signal(barrier, inc=1, device_id=(cut[0], jnp.where(is_z, 3 - 3 * xh, cut[1])), **mesh_id)
    pl.semaphore_signal(barrier, inc=1, device_id=(side[0], jnp.where(is_z, side[1], 3 * xh)), **mesh_id)

    @pl.when(jnp.logical_not(a_z))
    def _():
        pl.semaphore_signal(barrier, inc=1, device_id=sibling, **mesh_id)

    @pl.when(is_z)
    def _():
        for sign in (1, -1):
            pl.semaphore_signal(barrier, inc=1, device_id=(along_z(sign)[0], xh * 2 + 1 - xh), **mesh_id)

    acc[...] = jnp.zeros_like(acc)
    for load in loads:
        load.wait()

    @pl.when(jnp.logical_not(b_z))
    def _():
        pl.semaphore_wait(barrier, 3 + 2 * z)

    @pl.when(a_z)
    def _():
        pl.semaphore_signal(ready, inc=1, device_id=sibling, **mesh_id)

    @pl.when(b_z)
    def _():
        pl.semaphore_wait(ready, 1)

    def span(k):
        return pl.ds(pl.multiple_of(k * part, 16), part)

    def copy(flow, src, dst, peer, k):
        return pltpu.make_async_remote_copy(
            src_ref=buf.at[src, span(k)],
            dst_ref=buf.at[dst, span(k)],
            send_sem=send_sem.at[flow, k],
            recv_sem=recv_sem.at[dst, k],
            device_id=peer,
            **mesh_id,
        )

    def arrive(b, k):
        pltpu.make_async_copy(buf.at[b, span(k)], buf.at[b, span(k)], recv_sem.at[b, k]).wait()

    def sent(flow, k):
        pltpu.make_async_copy(buf.at[X, span(k)], buf.at[X, span(k)], send_sem.at[flow, k]).wait()

    second_from = jnp.where(is_z, ZIN, second_src)

    def each(body):
        lax.fori_loop(0, CHUNKS, lambda k, c: (body(k), c)[1], 0)

    def send_z(k):
        copy(F_Z, second_src, ZIN, along_z(z_second), k).start()

    @each
    def _(k):
        @pl.when(is_a)
        def _():
            copy(F_P1, first_src, TRANSIT, cut, k).start()

        @pl.when(is_b)
        def _():
            copy(F_P1, first_src, jnp.where(is_z, EXTRA, TRANSIT), side, k).start()

        @pl.when(jnp.logical_and(not_z, is_b))
        def _():
            copy(F_P2, second_from, D2, cut, k).start()

        copy(F_LOCAL, 1 - core, LOCAL, sibling, k).start()

    @pl.when(b_z)
    def _():
        pl.semaphore_wait(barrier, 4)
        pl.semaphore_signal(ready, inc=1, device_id=sibling, **mesh_id)
        each(send_z)

    def relay_a(k):
        held = jnp.where(is_z, TRANSIT, EXTRA)
        arrive(held, k)
        copy(F_RELAY, held, D1, cut, k).start()

        @pl.when(is_z)
        def _():
            copy(F_MZ, TRANSIT, EXTRA, along_z(z_extra), k).start()

    def relay_b(k):
        arrive(TRANSIT, k)
        copy(F_RELAY, TRANSIT, D1, side, k).start()

    def second_b(k):
        arrive(ZIN, k)
        copy(F_P2, ZIN, D2, cut, k).start()

    def second_a(k):
        @pl.when(is_z)
        def _():
            arrive(ZIN, k)

        copy(F_P2, second_from, D2, cut, k).start()
        copy(F_M2, second_from, EXTRA, side, k).start()

    factor = scale_ref[0] / math.sqrt(width)
    bias = bias_ref[0]

    def weigh(s, b, rows_of, own, offset=0):
        block = buf[b, rows_of, :]
        logits = lax.dot_general(buf[s], block, (((1,), (1,)), ((), ())), preferred_element_type=jnp.float32)
        weights = jax.nn.sigmoid(factor * logits + bias)
        if own is not None:
            row = lax.broadcasted_iota(jnp.int32, weights.shape, 0)
            column = lax.broadcasted_iota(jnp.int32, weights.shape, 1)
            weights = weights - (row == column + jnp.where(own, offset, rows)).astype(jnp.float32)
        acc[s] += jnp.dot(weights.astype(jnp.bfloat16), block, preferred_element_type=jnp.float32)

    def both(b, forward_flow):
        def one(k):
            arrive(b, k)
            copy(forward_flow, b, b + 1, sibling, k).start()

        return one

    forward_1, forward_2 = both(D1, F_D1), both(D2, F_D2)

    def arrive_half(b, h):
        for k in range(h * CHUNKS // 2, (h + 1) * CHUNKS // 2):
            arrive(b, k)

    def before(cond, number):
        return lambda body: plans.append((cond, number, body))

    plans = []

    @before(a_z, 2)
    def _():
        pl.semaphore_wait(ready, 1)
        each(send_z)

    @before(is_a, 2)
    def _():
        relay_a(0)

    @before(is_a, 4)
    def _():
        relay_a(1)

    @before(is_b, 4)
    def _():
        relay_b(0)

    @before(True, 4)
    def _():
        each(lambda k: arrive(LOCAL, k))

    @before(b_z, 5)
    def _():
        second_b(0)

    @before(is_a, 6)
    def _():
        relay_a(2)
        relay_a(3)

    @before(jnp.logical_and(is_a, not_z), 6)
    def _():
        each(second_a)

    @before(is_a, 6)
    def _():
        forward_1(0)
        forward_1(1)

    @before(b_n, 6)
    def _():
        relay_b(1)
        relay_b(2)
        relay_b(3)

    @before(b_z, 6)
    def _():
        relay_b(1)
        second_b(1)
        relay_b(2)
        relay_b(3)
        second_b(2)

    @before(is_b, 6)
    def _():
        arrive_half(D1F, 0)

    @before(a_z, 7)
    def _():
        arrive_half(EXTRA, 0)

    @before(is_a, 7)
    def _():
        forward_2(0)

    @before(b_z, 7)
    def _():
        arrive_half(EXTRA, 0)

    @before(b_n, 7)
    def _():
        arrive_half(D2F, 0)

    @before(a_z, 8)
    def _():
        second_a(0)
        second_a(1)

    @before(is_a, 8)
    def _():
        forward_2(1)

    @before(b_z, 8)
    def _():
        second_b(3)
        arrive_half(D2F, 0)

    @before(b_n, 8)
    def _():
        arrive_half(D1F, 1)

    @before(a_z, 9)
    def _():
        arrive_half(EXTRA, 1)
        second_a(2)

    @before(b_z, 9)
    def _():
        arrive_half(EXTRA, 1)

    @before(b_n, 9)
    def _():
        arrive_half(D2F, 1)

    @before(a_z, 10)
    def _():
        second_a(3)

    @before(is_a, 10)
    def _():
        forward_1(2)

    @before(is_a, 10)
    def _():
        forward_2(2)
        forward_1(3)

    @before(b_z, 10)
    def _():
        arrive_half(D1F, 1)

    @before(b_n, 10)
    def _():
        forward_1(0)
        forward_1(1)

    @before(is_a, 11)
    def _():
        forward_2(3)

    @before(b_z, 11)
    def _():
        forward_1(0)
        forward_1(1)

    @before(b_n, 11)
    def _():
        arrive_half(EXTRA, 0)

    @before(is_a, 12)
    def _():
        arrive_half(D1F, 0)

    @before(b_z, 12)
    def _():
        arrive_half(D2F, 1)

    @before(b_n, 12)
    def _():
        forward_1(2)
        forward_1(3)

    @before(is_a, 13)
    def _():
        arrive_half(D1F, 1)

    @before(b_z, 13)
    def _():
        forward_1(2)
        forward_1(3)

    @before(b_n, 13)
    def _():
        arrive_half(EXTRA, 1)

    first, second = 1 - xh, xh
    opening = [(Y, 0, 0), (Y, 1, 0), (X, 0, 1), (X, 1, 1)]
    units_a = opening + [(LOCAL, 0, first), (LOCAL, 1, first), (D1, 0, first), (EXTRA, 0, second),
                         (D2, 0, second), (EXTRA, 1, second), (D1, 1, first), (D2, 1, second),
                         (D1F, 0, first), (D1F, 1, first)]
    units_bz = opening + [(LOCAL, 0, second), (LOCAL, 1, second), (D1F, 0, first), (EXTRA, 0, first),
                          (D2F, 0, second), (EXTRA, 1, first), (D1F, 1, first), (D1, 0, first),
                          (D2F, 1, second), (D1, 1, first)]
    units_bn = opening + [(LOCAL, 0, second), (LOCAL, 1, second), (D1F, 0, first), (D2F, 0, second),
                          (D1F, 1, first), (D2F, 1, second), (D1, 0, first), (EXTRA, 0, first),
                          (D1, 1, first), (EXTRA, 1, first)]
    half = rows // 2

    def unit(u, carry):
        for cond, number, plan in plans:
            pl.when(jnp.logical_and(u == number, cond))(plan)

        def pick(field):
            value = jnp.int32(0)
            for number, (ua, ubz, ubn) in enumerate(zip(units_a, units_bz, units_bn)):
                which = jnp.where(is_a, ua[field], jnp.where(is_z, ubz[field], ubn[field]))
                value = jnp.where(u == number, which, value)
            return value

        h = pick(1)
        weigh(pick(2), pick(0), pl.ds(pl.multiple_of(h * half, 16), half), u < 4, h * half)
        return carry

    lax.fori_loop(0, len(units_a), unit, 0)
    acc[1 - xh] = acc[1 - xh] * factor

    @each
    def _(k):
        @pl.when(is_a)
        def _():
            arrive(D2F, k)

        @pl.when(is_b)
        def _():
            forward_2(k)

        @pl.when(k < CHUNKS - 1)
        def _():
            weigh(xh, D2 + a, span(k), None)

    @each
    def _(k):
        for flow in (F_LOCAL, F_P1, F_RELAY, F_P2, F_D1, F_D2):
            sent(flow, k)

        @pl.when(is_a)
        def _():
            sent(F_M2, k)

        @pl.when(is_z)
        def _():
            sent(F_Z, k)

        @pl.when(jnp.logical_and(is_z, is_a))
        def _():
            sent(F_MZ, k)


def finish(acc, buf, scale_ref, bias_ref, img_ref, txt_ref, result, sem):
    rows, width = img_ref.shape
    part = rows // CHUNKS
    tile = rows // TILES
    tensor = lax.axis_index("tensor")
    core, xh = lax.rem(tensor, 2), tensor // 2
    factor = scale_ref[0] / math.sqrt(width)
    bias = bias_ref[0]

    def write(src, dst, number):
        return pltpu.make_async_copy(src, dst, sem.at[number])

    def first(start):
        for s, ref in ((0, img_ref), (1, txt_ref)):
            @pl.when(xh == 1 - s)
            def _():
                c = write(acc.at[s], ref, 0)
                c.start() if start else c.wait()

    def second(m, start):
        span = pl.ds(m * tile, tile)
        for s, ref in ((0, img_ref), (1, txt_ref)):
            @pl.when(xh == s)
            def _():
                c = write(result.at[span], ref.at[span], 1 + m)
                c.start() if start else c.wait()

    first(True)
    block = buf[D2 + (core == xh).astype(jnp.int32), rows - part :, :]
    for m in range(TILES):
        span = pl.ds(m * tile, tile)
        logits = lax.dot_general(buf[xh, span, :], block, (((1,), (1,)), ((), ())), preferred_element_type=jnp.float32)
        weights = jax.nn.sigmoid(factor * logits + bias).astype(jnp.bfloat16)
        result[span, :] = factor * (acc[xh, span, :] + jnp.dot(weights, block, preferred_element_type=jnp.float32))
        second(m, True)
    first(False)
    for m in range(TILES):
        second(m, False)


def body(images, texts, logit_scale, logit_bias):
    rows, width = images.shape
    hbm = pl.BlockSpec(memory_space=pltpu.HBM)
    smem = pl.BlockSpec(memory_space=pltpu.SMEM)
    vmem = pl.BlockSpec(memory_space=pltpu.VMEM)
    out = jax.ShapeDtypeStruct((rows, width), jnp.float32)
    total, blocks = pl.pallas_call(
        functools.partial(kernel, lax.axis_size("dp")),
        out_shape=(pltpu.VMEM((2, rows, width), jnp.float32), pltpu.VMEM((10, rows, width), jnp.bfloat16)),
        in_specs=[hbm, hbm, smem, smem],
        out_specs=(vmem, vmem),
        scratch_shapes=[
            pltpu.SemaphoreType.DMA((2,)),
            pltpu.SemaphoreType.DMA((9, CHUNKS)),
            pltpu.SemaphoreType.DMA((10, CHUNKS)),
            pltpu.SemaphoreType.REGULAR,
        ],
        compiler_params=pltpu.CompilerParams(
            collective_id=0, has_side_effects=True, vmem_limit_bytes=41 << 20
        ),
        cost_estimate=pl.CostEstimate(
            flops=32 * rows * rows * width, bytes_accessed=12 * rows * width, transcendentals=8 * rows * rows
        ),
        name="pairs",
    )(images, texts, logit_scale, logit_bias)
    return pl.pallas_call(
        finish,
        out_shape=(out, out),
        in_specs=[vmem, vmem, smem, smem],
        out_specs=(hbm, hbm),
        scratch_shapes=[pltpu.VMEM((rows, width), jnp.float32), pltpu.SemaphoreType.DMA((1 + TILES,))],
        compiler_params=pltpu.CompilerParams(vmem_limit_bytes=41 << 20),
        name="finish",
    )(
        pltpu.with_memory_space_constraint(total, pltpu.VMEM),
        pltpu.with_memory_space_constraint(blocks, pltpu.VMEM),
        logit_scale,
        logit_bias,
    )


def solution(mesh):
    in_specs = (P(("dp", "tensor"), None), P(("dp", "tensor"), None), P(), P())
    out_specs = (P(("dp", "tensor"), None), P(("dp", "tensor"), None))
    return jax.shard_map(body, mesh=mesh, in_specs=in_specs, out_specs=out_specs, check_vma=False)
```

```python
import functools
import math

import jax
import jax.numpy as jnp
from jax import lax
from jax.experimental import pallas as pl
from jax.experimental.pallas import tpu as pltpu
from jax.sharding import PartitionSpec as P

CHUNKS = 4
TILES = 4
X, Y, LOCAL, D1, D1F, EXTRA, TRANSIT, ZIN, D2, D2F = range(10)
F_LOCAL, F_P1, F_RELAY, F_MZ, F_Z, F_P2, F_M2, F_D1, F_D2 = range(9)


def kernel(ndp, x_ref, y_ref, scale_ref, bias_ref, acc, buf, load_sem, send_sem, recv_sem, ready):
    rows, width = x_ref.shape
    part = rows // CHUNKS
    dp, tensor = lax.axis_index("dp"), lax.axis_index("tensor")
    core, xh, xl = lax.rem(tensor, 2), tensor // 2, lax.rem(dp, 2)
    is_a = core == xh
    is_z = xl == xh
    not_z = jnp.logical_not(is_z)
    is_b = jnp.logical_not(is_a)
    a = is_a.astype(jnp.int32)
    z = is_z.astype(jnp.int32)

    cut = (dp + 1 - 2 * xl, (1 - xh) * 2 + core)
    side = (dp + 1 - 2 * xl, xh * 2 + 1 - core)
    sibling = (dp, xh * 2 + 1 - core)

    def along_z(sign):
        return (lax.rem(dp + 2 * sign + ndp, ndp), tensor)

    z_extra = 1 - 2 * xh
    z_second = 2 * xh - 1
    first_src, second_src = 1 - xh, xh

    loads = [
        pltpu.make_async_copy(x_ref, buf.at[X], load_sem.at[0]),
        pltpu.make_async_copy(y_ref, buf.at[Y], load_sem.at[1]),
    ]
    for load in loads:
        load.start()
    mesh_id = dict(device_id_type=pl.DeviceIdType.MESH)
    barrier = pltpu.get_barrier_semaphore()
    a_z, b_z = jnp.logical_and(is_a, is_z), jnp.logical_and(is_b, is_z)
    b_n = jnp.logical_and(is_b, not_z)

    pl.semaphore_signal(barrier, inc=1, device_id=(cut[0], jnp.where(is_z, 3 - 3 * xh, cut[1])), **mesh_id)
    pl.semaphore_signal(barrier, inc=1, device_id=(side[0], jnp.where(is_z, side[1], 3 * xh)), **mesh_id)

    @pl.when(jnp.logical_not(a_z))
    def _():
        pl.semaphore_signal(barrier, inc=1, device_id=sibling, **mesh_id)

    @pl.when(is_z)
    def _():
        for sign in (1, -1):
            pl.semaphore_signal(barrier, inc=1, device_id=(along_z(sign)[0], xh * 2 + 1 - xh), **mesh_id)

    acc[...] = jnp.zeros_like(acc)

    @pl.when(jnp.logical_not(b_z))
    def _():
        pl.semaphore_wait(barrier, 3 + 2 * z)

    @pl.when(a_z)
    def _():
        pl.semaphore_signal(ready, inc=1, device_id=sibling, **mesh_id)

    @pl.when(b_z)
    def _():
        pl.semaphore_wait(ready, 1)

    def span(k):
        return pl.ds(pl.multiple_of(k * part, 16), part)

    def copy(flow, src, dst, peer, k):
        return pltpu.make_async_remote_copy(
            src_ref=buf.at[src, span(k)],
            dst_ref=buf.at[dst, span(k)],
            send_sem=send_sem.at[flow, k],
            recv_sem=recv_sem.at[dst, k],
            device_id=peer,
            **mesh_id,
        )

    def arrive(b, k):
        pltpu.make_async_copy(buf.at[b, span(k)], buf.at[b, span(k)], recv_sem.at[b, k]).wait()

    def sent(flow, k):
        pltpu.make_async_copy(buf.at[X, span(k)], buf.at[X, span(k)], send_sem.at[flow, k]).wait()

    second_from = jnp.where(is_z, ZIN, second_src)

    def each(body):
        lax.fori_loop(0, CHUNKS, lambda k, c: (body(k), c)[1], 0)

    def send_z(k):
        copy(F_Z, second_src, ZIN, along_z(z_second), k).start()

    def send_first(ref, k):
        def go(dst, peer):
            pltpu.make_async_remote_copy(
                src_ref=ref.at[span(k)],
                dst_ref=buf.at[dst, span(k)],
                send_sem=send_sem.at[F_P1, k],
                recv_sem=recv_sem.at[dst, k],
                device_id=peer,
                **mesh_id,
            ).start()

        pl.when(is_a)(lambda: go(TRANSIT, cut))
        pl.when(is_b)(lambda: go(jnp.where(is_z, EXTRA, TRANSIT), side))

    @each
    def _(k):
        pl.when(xh == 0)(lambda: send_first(y_ref, k))
        pl.when(xh == 1)(lambda: send_first(x_ref, k))

    for load in loads:
        load.wait()

    @each
    def _(k):
        @pl.when(jnp.logical_and(not_z, is_b))
        def _():
            copy(F_P2, second_from, D2, cut, k).start()

        copy(F_LOCAL, 1 - core, LOCAL, sibling, k).start()

    @pl.when(b_z)
    def _():
        pl.semaphore_wait(barrier, 4)
        pl.semaphore_signal(ready, inc=1, device_id=sibling, **mesh_id)
        each(send_z)

    def relay_a(k):
        held = jnp.where(is_z, TRANSIT, EXTRA)
        arrive(held, k)
        copy(F_RELAY, held, D1, cut, k).start()

        @pl.when(is_z)
        def _():
            copy(F_MZ, TRANSIT, EXTRA, along_z(z_extra), k).start()

    def relay_b(k):
        arrive(TRANSIT, k)
        copy(F_RELAY, TRANSIT, D1, side, k).start()

    def second_b(k):
        arrive(ZIN, k)
        copy(F_P2, ZIN, D2, cut, k).start()

    def second_a(k):
        @pl.when(is_z)
        def _():
            arrive(ZIN, k)

        copy(F_P2, second_from, D2, cut, k).start()
        copy(F_M2, second_from, EXTRA, side, k).start()

    factor = scale_ref[0] / math.sqrt(width)
    bias = bias_ref[0]

    def weigh(s, b, rows_of, own, offset=0):
        block = buf[b, rows_of, :]
        logits = lax.dot_general(buf[s], block, (((1,), (1,)), ((), ())), preferred_element_type=jnp.float32)
        weights = jax.nn.sigmoid(factor * logits + bias)
        if own is not None:
            row = lax.broadcasted_iota(jnp.int32, weights.shape, 0)
            column = lax.broadcasted_iota(jnp.int32, weights.shape, 1)
            weights = weights - (row == column + jnp.where(own, offset, rows)).astype(jnp.float32)
        acc[s] += jnp.dot(weights.astype(jnp.bfloat16), block, preferred_element_type=jnp.float32)

    def both(b, forward_flow):
        def one(k):
            arrive(b, k)
            copy(forward_flow, b, b + 1, sibling, k).start()

        return one

    forward_1, forward_2 = both(D1, F_D1), both(D2, F_D2)

    def arrive_half(b, h):
        for k in range(h * CHUNKS // 2, (h + 1) * CHUNKS // 2):
            arrive(b, k)

    def before(cond, number):
        return lambda body: plans.append((cond, number, body))

    plans = []

    @before(a_z, 2)
    def _():
        pl.semaphore_wait(ready, 1)
        each(send_z)

    @before(is_a, 2)
    def _():
        relay_a(0)

    @before(is_a, 4)
    def _():
        relay_a(1)

    @before(is_b, 4)
    def _():
        relay_b(0)

    @before(True, 4)
    def _():
        each(lambda k: arrive(LOCAL, k))

    @before(b_z, 5)
    def _():
        second_b(0)

    @before(is_a, 6)
    def _():
        relay_a(2)
        relay_a(3)

    @before(jnp.logical_and(is_a, not_z), 6)
    def _():
        each(second_a)

    @before(is_a, 6)
    def _():
        forward_1(0)
        forward_1(1)

    @before(b_n, 6)
    def _():
        relay_b(1)
        relay_b(2)
        relay_b(3)

    @before(b_z, 6)
    def _():
        relay_b(1)
        second_b(1)
        relay_b(2)
        relay_b(3)
        second_b(2)

    @before(is_b, 6)
    def _():
        arrive_half(D1F, 0)

    @before(a_z, 7)
    def _():
        arrive_half(EXTRA, 0)

    @before(is_a, 7)
    def _():
        forward_2(0)

    @before(b_z, 7)
    def _():
        arrive_half(EXTRA, 0)

    @before(b_n, 7)
    def _():
        arrive_half(D2F, 0)

    @before(a_z, 8)
    def _():
        second_a(0)
        second_a(1)

    @before(is_a, 8)
    def _():
        forward_2(1)

    @before(b_z, 8)
    def _():
        second_b(3)
        arrive_half(D2F, 0)

    @before(b_n, 8)
    def _():
        arrive_half(D1F, 1)

    @before(a_z, 9)
    def _():
        arrive_half(EXTRA, 1)
        second_a(2)

    @before(b_z, 9)
    def _():
        arrive_half(EXTRA, 1)

    @before(b_n, 9)
    def _():
        arrive_half(D2F, 1)

    @before(a_z, 10)
    def _():
        second_a(3)

    @before(is_a, 10)
    def _():
        forward_1(2)

    @before(is_a, 10)
    def _():
        forward_2(2)
        forward_1(3)

    @before(b_z, 10)
    def _():
        arrive_half(D1F, 1)

    @before(b_n, 10)
    def _():
        forward_1(0)
        forward_1(1)

    @before(is_a, 11)
    def _():
        forward_2(3)

    @before(b_z, 11)
    def _():
        forward_1(0)
        forward_1(1)

    @before(b_n, 11)
    def _():
        arrive_half(EXTRA, 0)

    @before(is_a, 12)
    def _():
        arrive_half(D1F, 0)

    @before(b_z, 12)
    def _():
        arrive_half(D2F, 1)

    @before(b_n, 12)
    def _():
        forward_1(2)
        forward_1(3)

    @before(is_a, 13)
    def _():
        arrive_half(D1F, 1)

    @before(b_z, 13)
    def _():
        forward_1(2)
        forward_1(3)

    @before(b_n, 13)
    def _():
        arrive_half(EXTRA, 1)

    first, second = 1 - xh, xh
    opening = [(Y, 0, 0), (Y, 1, 0), (X, 0, 1), (X, 1, 1)]
    units_a = opening + [(LOCAL, 0, first), (LOCAL, 1, first), (D1, 0, first), (EXTRA, 0, second),
                         (D2, 0, second), (EXTRA, 1, second), (D1, 1, first), (D2, 1, second),
                         (D1F, 0, first), (D1F, 1, first)]
    units_bz = opening + [(LOCAL, 0, second), (LOCAL, 1, second), (D1F, 0, first), (EXTRA, 0, first),
                          (D2F, 0, second), (EXTRA, 1, first), (D1F, 1, first), (D1, 0, first),
                          (D2F, 1, second), (D1, 1, first)]
    units_bn = opening + [(LOCAL, 0, second), (LOCAL, 1, second), (D1F, 0, first), (D2F, 0, second),
                          (D1F, 1, first), (D2F, 1, second), (D1, 0, first), (EXTRA, 0, first),
                          (D1, 1, first), (EXTRA, 1, first)]
    half = rows // 2

    def unit(u, carry):
        for cond, number, plan in plans:
            pl.when(jnp.logical_and(u == number, cond))(plan)

        def pick(field):
            value = jnp.int32(0)
            for number, (ua, ubz, ubn) in enumerate(zip(units_a, units_bz, units_bn)):
                which = jnp.where(is_a, ua[field], jnp.where(is_z, ubz[field], ubn[field]))
                value = jnp.where(u == number, which, value)
            return value

        h = pick(1)
        weigh(pick(2), pick(0), pl.ds(pl.multiple_of(h * half, 16), half), u < 4, h * half)
        return carry

    lax.fori_loop(0, len(units_a), unit, 0)
    acc[1 - xh] = acc[1 - xh] * factor

    @each
    def _(k):
        @pl.when(is_a)
        def _():
            arrive(D2F, k)

        @pl.when(is_b)
        def _():
            forward_2(k)

        @pl.when(k < CHUNKS - 1)
        def _():
            weigh(xh, D2 + a, span(k), None)

    @each
    def _(k):
        for flow in (F_LOCAL, F_P1, F_RELAY, F_P2, F_D1, F_D2):
            sent(flow, k)

        @pl.when(is_a)
        def _():
            sent(F_M2, k)

        @pl.when(is_z)
        def _():
            sent(F_Z, k)

        @pl.when(jnp.logical_and(is_z, is_a))
        def _():
            sent(F_MZ, k)


def finish(acc, buf, scale_ref, bias_ref, img_ref, txt_ref, result, sem):
    rows, width = img_ref.shape
    part = rows // CHUNKS
    tile = rows // TILES
    tensor = lax.axis_index("tensor")
    core, xh = lax.rem(tensor, 2), tensor // 2
    factor = scale_ref[0] / math.sqrt(width)
    bias = bias_ref[0]

    def write(src, dst, number):
        return pltpu.make_async_copy(src, dst, sem.at[number])

    def first(start):
        for s, ref in ((0, img_ref), (1, txt_ref)):
            @pl.when(xh == 1 - s)
            def _():
                c = write(acc.at[s], ref, 0)
                c.start() if start else c.wait()

    def second(m, start):
        span = pl.ds(m * tile, tile)
        for s, ref in ((0, img_ref), (1, txt_ref)):
            @pl.when(xh == s)
            def _():
                c = write(result.at[span], ref.at[span], 1 + m)
                c.start() if start else c.wait()

    first(True)
    block = buf[D2 + (core == xh).astype(jnp.int32), rows - part :, :]
    for m in range(TILES):
        span = pl.ds(m * tile, tile)
        logits = lax.dot_general(buf[xh, span, :], block, (((1,), (1,)), ((), ())), preferred_element_type=jnp.float32)
        weights = jax.nn.sigmoid(factor * logits + bias).astype(jnp.bfloat16)
        result[span, :] = factor * (acc[xh, span, :] + jnp.dot(weights, block, preferred_element_type=jnp.float32))
        second(m, True)
    first(False)
    for m in range(TILES):
        second(m, False)


def body(images, texts, logit_scale, logit_bias):
    rows, width = images.shape
    hbm = pl.BlockSpec(memory_space=pltpu.HBM)
    smem = pl.BlockSpec(memory_space=pltpu.SMEM)
    vmem = pl.BlockSpec(memory_space=pltpu.VMEM)
    out = jax.ShapeDtypeStruct((rows, width), jnp.float32)
    total, blocks = pl.pallas_call(
        functools.partial(kernel, lax.axis_size("dp")),
        out_shape=(pltpu.VMEM((2, rows, width), jnp.float32), pltpu.VMEM((10, rows, width), jnp.bfloat16)),
        in_specs=[hbm, hbm, smem, smem],
        out_specs=(vmem, vmem),
        scratch_shapes=[
            pltpu.SemaphoreType.DMA((2,)),
            pltpu.SemaphoreType.DMA((9, CHUNKS)),
            pltpu.SemaphoreType.DMA((10, CHUNKS)),
            pltpu.SemaphoreType.REGULAR,
        ],
        compiler_params=pltpu.CompilerParams(
            collective_id=0, has_side_effects=True, vmem_limit_bytes=41 << 20
        ),
        cost_estimate=pl.CostEstimate(
            flops=32 * rows * rows * width, bytes_accessed=12 * rows * width, transcendentals=8 * rows * rows
        ),
        name="pairs",
    )(images, texts, logit_scale, logit_bias)
    return pl.pallas_call(
        finish,
        out_shape=(out, out),
        in_specs=[vmem, vmem, smem, smem],
        out_specs=(hbm, hbm),
        scratch_shapes=[pltpu.VMEM((rows, width), jnp.float32), pltpu.SemaphoreType.DMA((1 + TILES,))],
        compiler_params=pltpu.CompilerParams(vmem_limit_bytes=41 << 20),
        name="finish",
    )(
        pltpu.with_memory_space_constraint(total, pltpu.VMEM),
        pltpu.with_memory_space_constraint(blocks, pltpu.VMEM),
        logit_scale,
        logit_bias,
    )


def solution(mesh):
    in_specs = (P(("dp", "tensor"), None), P(("dp", "tensor"), None), P(), P())
    out_specs = (P(("dp", "tensor"), None), P(("dp", "tensor"), None))
    return jax.shard_map(body, mesh=mesh, in_specs=in_specs, out_specs=out_specs, check_vma=False)
```
